256 devices in a mesh: gz: 64 (over z, x, core), gx: 4 (over y).
Axes of the slice: x: 4, y: 4, z: 8, core: 2. Of those that a mesh axis runs over, the one named last changes fastest.
Arguments:
- field: bfloat16 [128, 32, 256, 256], P('gz', None, 'gx'), may hold values from -6 to 6
- spectral_weight: bfloat16 [1024, 2, 32, 1024], P(('gz', 'gx')), may hold values from -1 to 1
- bypass_weight: bfloat16 [32, 32], replicated, may hold values from -1 to 1
- bypass_bias: float32 [32], replicated, may hold values from -1 to 1
Outputs:
- output: bfloat16 [128, 32, 256, 256], P('gz', None, 'gx')
The draws below stay inside these ranges and needn't reach their ends.
All inputs are finite; a program needn't handle non-finite values.
Results may differ from the reference program's by a relative error of at most 0.0044.
Values may be sent and summed in bfloat16 or wider, within the bound.
A program may use at most 128 MiB of HBM per device.

```python
import math
import jax
import jax.numpy as jnp
from jax import lax

C = 32
KX = 32
KY = 32
KZ = 32
NY = 256
CZ = 2
NZ = 128
NX = 256
PAIRS = 1024


def shard_levels(stream_key, shape, shards, least, largest):
    factor_of = 1.0
    for axis_at, blocks in shards:
        draws = jax.random.uniform(jax.random.fold_in(jax.random.fold_in(stream_key, 6), axis_at), (blocks,), jnp.float32, least / len(shards), largest / len(shards))
        factor_of = factor_of * jnp.repeat(jnp.exp(draws), shape[axis_at] // blocks).reshape((-1,) + (1,) * (len(shape) - 1 - axis_at))
    return factor_of


def bell_draw(key, dims, deviation, most, split=(), kind=jnp.bfloat16):
    level = shard_levels(key, dims, split, -0.22, 0.18) if split else 1.0
    values = jax.random.normal(key, dims, jnp.float32) * deviation * level
    return jnp.minimum(jnp.maximum(values, -most), most).astype(kind)


def setup_inputs(seed: int = 0) -> dict:
    key_list = jax.random.split(jax.random.key(seed), 5)
    field = bell_draw(key_list[0], (NZ, C, NX, NY), 1.0, 6.0, ((0, 64), (2, 4)))
    spectral_weight = bell_draw(key_list[1], (PAIRS, 2, C, KZ * C), C ** -0.5, 1.0, ((0, 256),))
    bypass_weight = bell_draw(key_list[2], (C, C), C ** -0.5, 1.0)
    bypass_bias = jnp.clip(jax.random.uniform(key_list[3], (C,), jnp.float32, -1.0, 1.0), -1.0, 1.0)
    return {"field": field, "spectral_weight": spectral_weight, "bypass_weight": bypass_weight, "bypass_bias": bypass_bias}


def mode_frequencies(modes_count):
    positions = jnp.arange(modes_count, dtype=jnp.int32)
    return jnp.where(positions < modes_count // 2, positions, positions - modes_count)

def phase_table(frequencies, places, length):
    phases = jnp.mod(frequencies[:, None] * places[None, :], length)
    angles = phases.astype(jnp.float32) * (2.0 * math.pi / length)
    return (jnp.cos(angles), jnp.sin(angles))

def pencil_spectrum(block, x_places, length_x):
    block_count, channels, width_x, width_y = block.shape
    cos_y, sin_y = phase_table(mode_frequencies(KY), jnp.arange(width_y, dtype=jnp.int32), width_y)
    table_y = jnp.concatenate([cos_y, -sin_y], axis=0).T.astype(jnp.bfloat16)
    along_y = jnp.dot(block.reshape(-1, width_y), table_y, preferred_element_type=jnp.float32)
    along_y = along_y.reshape(block_count, channels, width_x, 2, KY)
    real_y = along_y[:, :, :, 0]
    imag_y = along_y[:, :, :, 1]
    cos_x, sin_x = phase_table(mode_frequencies(KX), x_places, length_x)
    highest = lax.Precision.HIGHEST
    real_x = jnp.einsum('bcxa,kx->bakc', real_y, cos_x, precision=highest) + jnp.einsum('bcxa,kx->bakc', imag_y, sin_x, precision=highest)
    imag_x = jnp.einsum('bcxa,kx->bakc', imag_y, cos_x, precision=highest) - jnp.einsum('bcxa,kx->bakc', real_y, sin_x, precision=highest)
    return jnp.stack([real_x, imag_x], axis=0).reshape(2, block_count, KY * KX, channels)

def slab_spectrum(pencils, z_places, length_z):
    cos_z, sin_z = phase_table(jnp.arange(KZ, dtype=jnp.int32), z_places, length_z)
    highest = lax.Precision.HIGHEST
    real_part = jnp.einsum('kb,bqc->kqc', cos_z, pencils[0], precision=highest) + jnp.einsum('kb,bqc->kqc', sin_z, pencils[1], precision=highest)
    imag_part = jnp.einsum('kb,bqc->kqc', cos_z, pencils[1], precision=highest) - jnp.einsum('kb,bqc->kqc', sin_z, pencils[0], precision=highest)
    return jnp.stack([real_part, imag_part], axis=1)

def mix_modes(spectrum, weight):
    owned_pairs, two_parts, channels, wide = weight.shape
    full_weight = weight.astype(jnp.float32).reshape(owned_pairs, 2, channels, KZ, channels)
    highest = lax.Precision.HIGHEST
    weight_real = full_weight[:, 0]
    weight_imag = full_weight[:, 1]
    spec_real = spectrum[:, 0]
    spec_imag = spectrum[:, 1]
    mixed_real = jnp.einsum('kqi,qiko->kqo', spec_real, weight_real, precision=highest) - jnp.einsum('kqi,qiko->kqo', spec_imag, weight_imag, precision=highest)
    mixed_imag = jnp.einsum('kqi,qiko->kqo', spec_real, weight_imag, precision=highest) + jnp.einsum('kqi,qiko->kqo', spec_imag, weight_real, precision=highest)
    return jnp.stack([mixed_real, mixed_imag], axis=1).astype(jnp.bfloat16)

def plane_values(mixed_modes, z_places, length_z):
    frequencies = jnp.arange(KZ, dtype=jnp.int32)
    factors = jnp.where(frequencies == 0, 1.0, 2.0) / (2.0 * math.sqrt(KX * KY * KZ))
    cos_z, sin_z = phase_table(frequencies, z_places, length_z)
    cos_z = cos_z * factors[:, None]
    sin_z = sin_z * factors[:, None]
    mode_real = mixed_modes[:, 0].astype(jnp.float32)
    mode_imag = mixed_modes[:, 1].astype(jnp.float32)
    highest = lax.Precision.HIGHEST
    real_part = jnp.einsum('kz,kqc->zqc', cos_z, mode_real, precision=highest) - jnp.einsum('kz,kqc->zqc', sin_z, mode_imag, precision=highest)
    imag_part = jnp.einsum('kz,kqc->zqc', sin_z, mode_real, precision=highest) + jnp.einsum('kz,kqc->zqc', cos_z, mode_imag, precision=highest)
    return jnp.stack([real_part, imag_part], axis=1)

def grid_values(planes, x_places, length_x):
    plane_count = planes.shape[0]
    channels = planes.shape[3]
    shaped = planes.reshape(plane_count, 2, KY, KX, channels)
    cos_x, sin_x = phase_table(mode_frequencies(KX), x_places, length_x)
    highest = lax.Precision.HIGHEST
    real_h = jnp.einsum('zakc,kx->zcxa', shaped[:, 0], cos_x, precision=highest) - jnp.einsum('zakc,kx->zcxa', shaped[:, 1], sin_x, precision=highest)
    imag_h = jnp.einsum('zakc,kx->zcxa', shaped[:, 0], sin_x, precision=highest) + jnp.einsum('zakc,kx->zcxa', shaped[:, 1], cos_x, precision=highest)
    cos_y, sin_y = phase_table(mode_frequencies(KY), jnp.arange(NY, dtype=jnp.int32), NY)
    table_y = jnp.concatenate([cos_y, -sin_y], axis=0)
    joined = jnp.concatenate([real_h, imag_h], axis=-1)
    width_x = joined.shape[2]
    values = jnp.dot(joined.reshape(-1, 2 * KY), table_y, precision=highest)
    return values.reshape(plane_count, channels, width_x, NY)

def finish(block, values, bypass_weight, bypass_bias):
    direct = jnp.einsum('zcxy,cd->zdxy', block.astype(jnp.float32), bypass_weight.astype(jnp.float32))
    total = values + direct + bypass_bias[None, :, None, None]
    return jax.nn.gelu(total, approximate=False).astype(jnp.bfloat16)

def reference(field, spectral_weight, bypass_weight, bypass_bias):
    block_total = NZ // CZ
    blocks = field.reshape(block_total, CZ, C, NX, NY)
    x_places = jnp.arange(NX, dtype=jnp.int32)
    pencils = lax.map(lambda block: pencil_spectrum(block, x_places, NX), blocks)
    pencils = pencils.transpose(1, 0, 2, 3, 4).reshape(2, NZ, PAIRS, C)
    forward_scale = 1.0 / math.sqrt(NX * NY * NZ)
    spectrum = slab_spectrum(pencils, jnp.arange(NZ, dtype=jnp.int32), NZ) * forward_scale
    mixed_modes = mix_modes(spectrum, spectral_weight)
    starts = jnp.arange(block_total, dtype=jnp.int32) * CZ

    def one_block(inputs):
        block, start = inputs
        z_places = start + jnp.arange(CZ, dtype=jnp.int32)
        planes = plane_values(mixed_modes, z_places, NZ)
        values = grid_values(planes, x_places, NX)
        return finish(block, values, bypass_weight, bypass_bias)
    result = lax.map(one_block, (blocks, starts))
    return result.reshape(NZ, C, NX, NY)
```

```python
import math

import jax
import jax.numpy as jnp
import ml_dtypes
import numpy as np
from jax import lax
from jax.experimental import pallas as pl
from jax.experimental.pallas import tpu as pltpu
from jax.sharding import PartitionSpec as P

NX, NY, NZ = 256, 256, 128
BF16 = jnp.bfloat16
F32 = jnp.float32
MESH = pl.DeviceIdType.MESH
NT = (((1,), (1,)), ((), ()))
TN = (((0,), (0,)), ((), ()))


def split(table):
    high = table.astype(ml_dtypes.bfloat16)
    low = (table - high.astype(np.float64)).astype(ml_dtypes.bfloat16)
    return high, low


def wave(frequency, place, length):
    angle = 2.0 * math.pi * np.mod(frequency * place, length) / length
    return np.cos(angle), np.sin(angle)


def signed(mode):
    return np.where(mode < 16, mode, mode - 32)


def axes(*sizes):
    return np.meshgrid(*[np.arange(size) for size in sizes], indexing="ij")


def one_hot(rows, columns, size):
    table = np.zeros((size, size), np.float64)
    table[rows.reshape(-1), columns.reshape(-1)] = 1.0
    return table.astype(ml_dtypes.bfloat16)


def forward_x():
    gx, px, hi, j, c, cc, x = axes(4, 2, 8, 4, 4, 4, 64)
    cos, sin = wave(signed(4 * hi + j), 64 * gx + x, NX)
    table = np.where(px == 0, cos, -sin) * (c == cc)
    return np.stack(split(table.reshape(4, 256, 256)), axis=1)


def forward_y():
    xd, part, zd, px, y = axes(4, 2, 8, 2, NY)
    cos, sin = wave(signed(4 * zd + xd), y, NY)
    table = np.where(px == part, cos, np.where(part == 0, sin, -sin))
    return table.reshape(64, 2 * NY).astype(ml_dtypes.bfloat16)


def order_to_owner():
    xs, b, core, part, zd = axes(4, 2, 2, 2, 8)
    source = (((xs * 2 + b) * 2 + core) * 2 + part) * 8 + zd
    target = (((zd * 2 + core) * 4 + xs) * 2 + b) * 2 + part
    return one_hot(target, source, 256)


def order_to_grid():
    xs, b, core, part, zs = axes(4, 2, 2, 2, 8)
    target = (((xs * 2 + b) * 2 + core) * 2 + part) * 8 + zs
    source = (((zs * 2 + core) * 4 + xs) * 2 + b) * 2 + part
    return one_hot(target, source, 256)


def order_channels():
    j, i = axes(4, 32)
    return one_hot(j * 32 + i, (i // 4) * 16 + j * 4 + i % 4, 128)


def forward_z():
    zs, core, xs, b, part, part_out, kz, o = axes(8, 2, 4, 2, 2, 2, 32, 32)
    cos, sin = wave(kz, 16 * zs + 4 * xs + 2 * core + b, NZ)
    table = np.where(part == part_out, cos, np.where(part_out == 0, sin, -sin)) / math.sqrt(NX * NY * NZ)
    return np.stack(split(table.reshape(256, 2048)))


def turn_lanes():
    table = np.zeros((128, 4, 128), np.float64)
    turn, low, o = axes(4, 4, 32)
    j = (low + turn) % 4
    table[low * 32 + o, turn, (o // 4) * 16 + j * 4 + o % 4] = 1.0
    return table.reshape(128, 512).astype(ml_dtypes.bfloat16)


def inverse_z():
    zd, core, xd, b, part_out, turn, high, part, j = axes(8, 2, 4, 2, 2, 4, 8, 2, 4)
    kz = 4 * high + (j - turn) % 4
    cos, sin = wave(kz, 16 * zd + 4 * xd + 2 * core + b, NZ)
    table = np.where(part == part_out, cos, np.where(part_out == 0, -sin, sin))
    table = table * np.where(kz == 0, 1.0, 2.0) / (2.0 * math.sqrt(32 * 32 * 32))
    return np.stack(split(table.reshape(256, 256)))


def inverse_y():
    xs, part, zs, part_out, y = axes(4, 2, 8, 2, NY)
    cos, sin = wave(signed(4 * zs + xs), y, NY)
    table = np.where(part == part_out, cos, np.where(part_out == 0, -sin, sin))
    return np.concatenate(split(table.reshape(64, 2 * NY)))


def inverse_x():
    gx, group, o, x, part, hi, j, oo = axes(4, 4, 4, 16, 2, 8, 4, 4)
    cos, sin = wave(signed(4 * hi + j), 64 * gx + 16 * group + x, NX)
    table = np.where(part == 0, cos, -sin) * (o == oo)
    return np.concatenate(split(table.reshape(4, 4, 64, 256)), axis=2)


def forward_kernel(field_ref, table_x_ref, table_y_ref, out_ref, field, table_x, along, sems):
    gx = lax.axis_index("gx")
    fetch_x = pltpu.make_async_copy(table_x_ref.at[gx], table_x, sems.at[4])
    fetch_x.start()
    fetches = []
    for part in range(4):
        b, half = part // 2, part % 2
        fetch = pltpu.make_async_copy(
            field_ref.at[b, pl.ds(16 * half, 16)], field.at[part], sems.at[part]
        )
        fetch.start()
        fetches.append(fetch)
    fetch_x.wait()
    for part in range(4):
        b, half = part // 2, part % 2
        fetches[part].wait()
        for inner in range(4):
            group = 4 * half + inner
            block = field[part, 4 * inner : 4 * inner + 4].reshape(256, NY)
            modes = jnp.dot(table_x[0], block, preferred_element_type=F32)
            modes += jnp.dot(table_x[1], block, preferred_element_type=F32)
            modes = modes.astype(BF16)
            for px in range(2):
                for hi in range(8):
                    row = (b * 8 + hi) * 128 + group * 16
                    at = (px * 8 + hi) * 16
                    along[row : row + 16, px * NY : (px + 1) * NY] = modes[at : at + 16]
    for b in range(2):
        for core in range(2):
            row = (b * 2 + core) * 512
            pencil = lax.dot_general(
                table_y_ref[...], along[row : row + 512], NT, preferred_element_type=F32
            ).astype(BF16)
            at = (b * 2 + core) * 16
            for xd in range(4):
                for yd in range(4):
                    out_ref[xd * 4 + yd, at : at + 16, :] = pencil[
                        xd * 16 : xd * 16 + 16, yd * 128 : yd * 128 + 128
                    ]


def exchange_kernel(
    send_ref, weight_ref, to_owner_ref, channels_ref, table_z_ref, turn_ref, back_z_ref, to_grid_ref,
    out_ref,
    got_a, send_b, got_b, back_b, home_b, back_a,
    weight, to_owner, channels, table_z, turn, back_z, to_grid,
    sems, send_sems, recv_sems,
):
    gz = lax.axis_index("gz")
    y = lax.axis_index("gx")
    core = lax.rem(gz, 2)
    x = lax.rem(lax.div(gz, 2), 4)
    z = lax.div(gz, 8)

    def plane_device(index):
        return ((z * 4 + lax.div(index, 4)) * 2 + core, lax.rem(index, 4))

    def line_device(index):
        return ((lax.div(index, 2) * 4 + x) * 2 + lax.rem(index, 2), y)

    plane_me = x * 4 + y
    line_me = z * 2 + core
    arrival = y * 4 + x

    barrier = pltpu.get_barrier_semaphore()

    def greet(step, carry):
        pl.semaphore_signal(
            barrier, inc=1, device_id=plane_device(lax.rem(plane_me + step, 16)), device_id_type=MESH
        )
        pl.semaphore_signal(
            barrier, inc=1, device_id=line_device(lax.rem(line_me + step, 16)), device_id_type=MESH
        )
        return carry

    lax.fori_loop(1, 16, greet, 0)

    fetches = []
    for at, (source, target) in enumerate(
        (
            (to_owner_ref, to_owner), (channels_ref, channels), (table_z_ref, table_z),
            (weight_ref, weight), (turn_ref, turn), (back_z_ref, back_z), (to_grid_ref, to_grid),
        )
    ):
        fetch = pltpu.make_async_copy(source, target, sems.at[at])
        fetch.start()
        fetches.append(fetch)

    got_a[arrival] = send_ref[plane_me]
    pl.semaphore_wait(barrier, 30)

    def plane_copy(phase, index, source, target):
        return pltpu.make_async_remote_copy(
            src_ref=source, dst_ref=target,
            send_sem=send_sems.at[phase, index], recv_sem=recv_sems.at[phase, arrival],
            device_id=plane_device(index), device_id_type=MESH,
        )

    def line_copy(phase, index, source, target):
        return pltpu.make_async_remote_copy(
            src_ref=source, dst_ref=target,
            send_sem=send_sems.at[phase, index], recv_sem=recv_sems.at[phase, line_me],
            device_id=line_device(index), device_id_type=MESH,
        )

    def arrived(phase, index, block):
        pltpu.make_async_copy(block, block, recv_sems.at[phase, index]).wait()

    def each(body):
        lax.fori_loop(1, 16, lambda step, carry: (body(step), carry)[1], 0)

    def send_plane(step):
        index = lax.rem(plane_me + step, 16)
        plane_copy(0, index, send_ref.at[index], got_a.at[arrival]).start()

    each(send_plane)

    def take_plane(step):
        index = lax.rem(arrival + step, 16)
        arrived(0, index, got_a.at[index])

    each(take_plane)
    fetches[0].wait()
    summed = jnp.zeros((256, 128), F32)
    for sy in range(4):
        summed += jnp.dot(
            to_owner[...], got_a[sy * 4 : sy * 4 + 4].reshape(256, 128), preferred_element_type=F32
        )
    send_b[...] = summed.astype(BF16).reshape(16, 16, 128)

    got_b[line_me] = send_b[line_me]

    def send_line(step):
        index = lax.rem(line_me + step, 16)
        line_copy(1, index, send_b.at[index], got_b.at[line_me]).start()

    each(send_line)
    for fetch in fetches[1:]:
        fetch.wait()

    def take_line(step):
        index = lax.rem(line_me + step, 16)
        arrived(1, index, got_b.at[index])

    each(take_line)
    pencils = lax.dot_general(
        channels[...], got_b[...].reshape(256, 128), NT, preferred_element_type=F32
    ).astype(BF16)
    rows = []
    for part in range(2):
        for j in range(4):
            rows.append([])
    for block in range(4):
        real_at, imag_at = block * 256, 1024 + block * 256
        real = jnp.dot(pencils, table_z[0, :, real_at : real_at + 256], preferred_element_type=F32)
        real += jnp.dot(pencils, table_z[1, :, real_at : real_at + 256], preferred_element_type=F32)
        imag = jnp.dot(pencils, table_z[0, :, imag_at : imag_at + 256], preferred_element_type=F32)
        imag += jnp.dot(pencils, table_z[1, :, imag_at : imag_at + 256], preferred_element_type=F32)
        for j in range(4):
            weight_real = weight[j, 0, :, real_at : real_at + 256].astype(F32)
            weight_imag = weight[j, 1, :, real_at : real_at + 256].astype(F32)
            one, two = real[j * 32 : j * 32 + 32], imag[j * 32 : j * 32 + 32]
            rows[j].append(jnp.sum(one * weight_real - two * weight_imag, axis=0, keepdims=True))
            rows[4 + j].append(jnp.sum(one * weight_imag + two * weight_real, axis=0, keepdims=True))
    mixed = jnp.concatenate([jnp.concatenate(row, axis=1) for row in rows], axis=0).astype(BF16)
    mixed = jnp.concatenate([mixed[:, h * 128 : h * 128 + 128].astype(F32) for h in range(8)], axis=0)
    turned = jnp.dot(mixed.astype(BF16), turn[...], preferred_element_type=F32)
    turned = jnp.concatenate([turned[:, t * 128 : t * 128 + 128] for t in range(4)], axis=0)
    row = lax.broadcasted_iota(jnp.int32, (256, 128), 0)
    lane = lax.broadcasted_iota(jnp.int32, (256, 128), 1)
    turned = jnp.where(lax.rem(row, 4) == lax.rem(lax.div(lane, 4), 4), turned, 0.0).astype(BF16)
    planes = jnp.dot(back_z[0], turned, preferred_element_type=F32)
    planes += jnp.dot(back_z[1], turned, preferred_element_type=F32)
    back_b[...] = planes.astype(BF16).reshape(16, 16, 128)

    home_b[line_me] = back_b[line_me]

    def return_line(step):
        index = lax.rem(line_me + step, 16)
        line_copy(2, index, back_b.at[index], home_b.at[line_me]).start()

    each(return_line)

    def home_line(step):
        index = lax.rem(line_me + step, 16)
        arrived(2, index, home_b.at[index])

    each(home_line)
    home = jnp.dot(to_grid[...], home_b[...].reshape(256, 128), preferred_element_type=F32)
    back_a[...] = home.astype(BF16).reshape(4, 64, 128)

    out_ref[arrival] = back_a[x]

    def return_plane(step):
        index = lax.rem(plane_me + step, 16)
        plane_copy(3, index, back_a.at[lax.div(index, 4)], out_ref.at[arrival]).start()

    each(return_plane)

    def home_plane(step):
        index = lax.rem(arrival + step, 16)
        arrived(3, index, out_ref.at[index])

    each(home_plane)

    def sent(step):
        plane_index = lax.rem(plane_me + step, 16)
        line_index = lax.rem(line_me + step, 16)
        plane_copy(0, plane_index, send_ref.at[plane_index], got_a.at[arrival]).wait_send()
        line_copy(1, line_index, send_b.at[line_index], got_b.at[line_me]).wait_send()
        line_copy(2, line_index, back_b.at[line_index], home_b.at[line_me]).wait_send()
        plane_copy(
            3, plane_index, back_a.at[lax.div(plane_index, 4)], out_ref.at[arrival]
        ).wait_send()

    each(sent)


def grid_kernel(
    modes_ref, field_ref, table_y_ref, table_x_ref, bypass_ref, bias_ref, out_ref,
    along, direct_table, bias, table_x, sem,
):
    b, group = pl.program_id(0), pl.program_id(1)

    @pl.when((b == 0) & (group == 0))
    def _():
        gx = lax.axis_index("gx")
        fetch = pltpu.make_async_copy(table_x_ref.at[gx], table_x, sem)
        fetch.start()
        row = lax.div(lax.broadcasted_iota(jnp.int32, (512, 32), 0), 16)
        lane = lax.broadcasted_iota(jnp.int32, (512, 32), 1)
        spread = (row == lane).astype(F32)
        bias[...] = jnp.sum(spread * bias_ref[...], axis=1, keepdims=True)
        spread = spread.astype(BF16)
        wide = lax.dot_general(spread, bypass_ref[...], NT, preferred_element_type=F32).astype(BF16)
        wide = lax.dot_general(wide, spread, NT, preferred_element_type=F32)
        one = lax.rem(lax.broadcasted_iota(jnp.int32, (512, 512), 0), 16)
        two = lax.rem(lax.broadcasted_iota(jnp.int32, (512, 512), 1), 16)
        direct_table[...] = jnp.where(one == two, wide, 0.0).astype(BF16)
        fetch.wait()

    @pl.when(group == 0)
    def _():
        for core in range(2):
            for ys in range(4):
                rows = modes_ref[ys * 4 : ys * 4 + 4, pl.ds(b * 32 + core * 16, 16), :].reshape(64, 128)
                rows = jnp.concatenate([rows, rows], axis=0)
                lines = lax.dot_general(rows, table_y_ref[...], TN, preferred_element_type=F32)
                lines = lines.astype(BF16)
                for part in range(2):
                    at = (part * 8 + core * 4 + ys) * 16
                    for channel in range(8):
                        along[channel, at : at + 16, :] = lines[
                            channel * 16 : channel * 16 + 16, part * NY : (part + 1) * NY
                        ]

    direct = jnp.dot(
        direct_table[...], field_ref[0].reshape(512, NY), preferred_element_type=F32
    )
    for channel in range(8):
        values = jnp.dot(table_x[group], along[channel], preferred_element_type=F32)
        at = channel * 64
        total = values[:64] + values[64:] + direct[at : at + 64] + bias[at : at + 64]
        result = 0.5 * total * (1.0 + lax.erf(total * (1.0 / math.sqrt(2.0))))
        out_ref[0, channel * 4 : channel * 4 + 4] = result.astype(BF16).reshape(4, 16, NY)


VMEM = pl.BlockSpec(memory_space=pltpu.VMEM)
ANY = pl.BlockSpec(memory_space=pl.ANY)


def shards(field, spectral_weight, bypass_weight, bypass_bias):
    pencils = pl.pallas_call(
        forward_kernel,
        out_shape=jax.ShapeDtypeStruct((16, 64, 128), BF16),
        in_specs=[ANY, ANY, VMEM],
        out_specs=VMEM,
        scratch_shapes=[
            pltpu.VMEM((4, 16, 64, NY), BF16),
            pltpu.VMEM((2, 256, 256), BF16),
            pltpu.VMEM((2048, 2 * NY), BF16),
            pltpu.SemaphoreType.DMA((5,)),
        ],
        compiler_params=pltpu.CompilerParams(vmem_limit_bytes=24 << 20),
        name="forward",
    )(field, jnp.asarray(forward_x()), jnp.asarray(forward_y()))

    modes = pl.pallas_call(
        exchange_kernel,
        out_shape=jax.ShapeDtypeStruct((16, 64, 128), BF16),
        in_specs=[VMEM] + [ANY] * 7,
        out_specs=VMEM,
        scratch_shapes=[
            pltpu.VMEM((16, 64, 128), BF16),
            pltpu.VMEM((16, 16, 128), BF16),
            pltpu.VMEM((16, 16, 128), BF16),
            pltpu.VMEM((16, 16, 128), BF16),
            pltpu.VMEM((16, 16, 128), BF16),
            pltpu.VMEM((4, 64, 128), BF16),
            pltpu.VMEM((4, 2, 32, 1024), BF16),
            pltpu.VMEM((256, 256), BF16),
            pltpu.VMEM((128, 128), BF16),
            pltpu.VMEM((2, 256, 2048), BF16),
            pltpu.VMEM((128, 512), BF16),
            pltpu.VMEM((2, 256, 256), BF16),
            pltpu.VMEM((256, 256), BF16),
            pltpu.SemaphoreType.DMA((7,)),
            pltpu.SemaphoreType.DMA((4, 16)),
            pltpu.SemaphoreType.DMA((4, 16)),
        ],
        compiler_params=pltpu.CompilerParams(
            collective_id=0, has_side_effects=True, vmem_limit_bytes=24 << 20
        ),
        name="exchange",
    )(
        pencils, spectral_weight, jnp.asarray(order_to_owner()), jnp.asarray(order_channels()),
        jnp.asarray(forward_z()), jnp.asarray(turn_lanes()), jnp.asarray(inverse_z()),
        jnp.asarray(order_to_grid()),
    )

    block = pl.BlockSpec((1, 32, 16, NY), lambda b, group: (b, 0, group, 0))
    return pl.pallas_call(
        grid_kernel,
        grid=(2, 4),
        out_shape=jax.ShapeDtypeStruct(field.shape, BF16),
        in_specs=[VMEM, block, VMEM, ANY, VMEM, VMEM],
        out_specs=block,
        scratch_shapes=[
            pltpu.VMEM((8, 256, NY), BF16),
            pltpu.VMEM((512, 512), BF16),
            pltpu.VMEM((512, 1), F32),
            pltpu.VMEM((4, 128, 256), BF16),
            pltpu.SemaphoreType.DMA,
        ],
        compiler_params=pltpu.CompilerParams(vmem_limit_bytes=24 << 20),
        name="grid",
    )(
        modes, field, jnp.asarray(inverse_y()), jnp.asarray(inverse_x()), bypass_weight,
        bypass_bias.reshape(1, 32),
    )


def solution(mesh):
    in_specs = (P("gz", None, "gx", None), P(("gz", "gx"), None, None, None), P(), P())
    out_specs = P("gz", None, "gx", None)
    return jax.shard_map(shards, mesh=mesh, in_specs=in_specs, out_specs=out_specs, check_vma=False)
```

```python
import math

import jax
import jax.numpy as jnp
import ml_dtypes
import numpy as np
from jax import lax
from jax.experimental import pallas as pl
from jax.experimental.pallas import tpu as pltpu
from jax.sharding import PartitionSpec as P

NX, NY, NZ = 256, 256, 128
BF16 = jnp.bfloat16
F32 = jnp.float32
MESH = pl.DeviceIdType.MESH
NT = (((1,), (1,)), ((), ()))
TN = (((0,), (0,)), ((), ()))


PLANE = [(dx, dy) for dx in range(4) for dy in range(4) if dx or dy]
LINE = [(dz, dc) for dz in range(8) for dc in range(2) if dz or dc]


def ring(step, size):
    return min(step, size - step)


def split(table):
    high = table.astype(ml_dtypes.bfloat16)
    low = (table - high.astype(np.float64)).astype(ml_dtypes.bfloat16)
    return high, low


def wave(frequency, place, length):
    angle = 2.0 * math.pi * np.mod(frequency * place, length) / length
    return np.cos(angle), np.sin(angle)


def signed(mode):
    return np.where(mode < 16, mode, mode - 32)


def axes(*sizes):
    return np.meshgrid(*[np.arange(size) for size in sizes], indexing="ij")


def one_hot(rows, columns, size):
    table = np.zeros((size, size), np.float64)
    table[rows.reshape(-1), columns.reshape(-1)] = 1.0
    return table.astype(ml_dtypes.bfloat16)


def forward_x():
    gx, px, hi, j, c, cc, x = axes(4, 2, 8, 4, 4, 4, 64)
    cos, sin = wave(signed(4 * hi + j), 64 * gx + x, NX)
    table = np.where(px == 0, cos, -sin) * (c == cc)
    return np.stack(split(table.reshape(4, 256, 256)), axis=1)


def forward_y():
    xd, part, zd, px, y = axes(4, 2, 8, 2, NY)
    cos, sin = wave(signed(4 * zd + xd), y, NY)
    table = np.where(px == part, cos, np.where(part == 0, sin, -sin))
    return table.reshape(64, 2 * NY).astype(ml_dtypes.bfloat16)


def order_to_owner():
    xs, b, core, part, zd = axes(4, 2, 2, 2, 8)
    source = (((xs * 2 + b) * 2 + core) * 2 + part) * 8 + zd
    target = (((zd * 2 + core) * 4 + xs) * 2 + b) * 2 + part
    return one_hot(target, source, 256)


def order_to_grid():
    xs, b, core, part, zs = axes(4, 2, 2, 2, 8)
    target = (((xs * 2 + b) * 2 + core) * 2 + part) * 8 + zs
    source = (((zs * 2 + core) * 4 + xs) * 2 + b) * 2 + part
    return one_hot(target, source, 256)


def order_channels():
    j, i = axes(4, 32)
    return one_hot(j * 32 + i, (i // 4) * 16 + j * 4 + i % 4, 128)


def forward_z():
    zs, core, xs, b, part, part_out, kz, o = axes(8, 2, 4, 2, 2, 2, 32, 32)
    cos, sin = wave(kz, 16 * zs + 4 * xs + 2 * core + b, NZ)
    table = np.where(part == part_out, cos, np.where(part_out == 0, sin, -sin)) / math.sqrt(NX * NY * NZ)
    return np.stack(split(table.reshape(256, 2048)))


def turn_lanes():
    table = np.zeros((128, 4, 128), np.float64)
    turn, low, o = axes(4, 4, 32)
    j = (low + turn) % 4
    table[low * 32 + o, turn, (o // 4) * 16 + j * 4 + o % 4] = 1.0
    return table.reshape(128, 512).astype(ml_dtypes.bfloat16)


def inverse_z():
    zd, core, xd, b, part_out, turn, high, part, j = axes(8, 2, 4, 2, 2, 4, 8, 2, 4)
    kz = 4 * high + (j - turn) % 4
    cos, sin = wave(kz, 16 * zd + 4 * xd + 2 * core + b, NZ)
    table = np.where(part == part_out, cos, np.where(part_out == 0, -sin, sin))
    table = table * np.where(kz == 0, 1.0, 2.0) / (2.0 * math.sqrt(32 * 32 * 32))
    return np.stack(split(table.reshape(256, 256)))


def inverse_y():
    xs, part, zs, part_out, y = axes(4, 2, 8, 2, NY)
    cos, sin = wave(signed(4 * zs + xs), y, NY)
    table = np.where(part == part_out, cos, np.where(part_out == 0, -sin, sin))
    return np.concatenate(split(table.reshape(64, 2 * NY)))


def inverse_x():
    gx, o, x, part, hi, j, oo = axes(4, 4, 64, 2, 8, 4, 4)
    cos, sin = wave(signed(4 * hi + j), 64 * gx + x, NX)
    table = np.where(part == 0, cos, -sin) * (o == oo)
    return np.concatenate(split(table.reshape(4, 256, 256)), axis=1)


def exchange_kernel(
    field_ref, table_x_ref, table_y_ref, weight_ref, to_owner_ref, channels_ref, table_z_ref, turn_ref,
    back_z_ref, to_grid_ref, back_y_ref, back_x_ref, bypass_ref, bias_ref,
    out_ref,
    send_a, got_a, send_b, got_b, back_b, home_b, back_a, home_a,
    field, table_x, table_y, along, weight, to_owner, channels, table_z, turn, back_z, to_grid,
    back_y, back_x, direct_table, direct, lines, result,
    sems, send_sems, recv_sems, store_sems,
):
    gz = lax.axis_index("gz")
    y = lax.axis_index("gx")
    core = gz & 1
    x = lax.shift_right_logical(gz, 1) & 3
    z = lax.shift_right_logical(gz, 3)
    xs = [(x + step) & 3 for step in range(4)]
    ys = [(y + step) & 3 for step in range(4)]
    zs = [(z + step) & 7 for step in range(8)]
    cores = [core, 1 - core]

    plane = []
    for dx, dy in sorted(PLANE, key=lambda step: -ring(step[0], 4) - ring(step[1], 4)):
        plane.append((xs[dx] * 4 + ys[dy], ys[dy] * 4 + xs[dx], (z * 8 + xs[dx] * 2 + core, ys[dy])))
    line = []
    for dz, dc in sorted(LINE, key=lambda step: -ring(step[0], 8) - 0.1 * step[1]):
        line.append((zs[dz] * 2 + cores[dc], (zs[dz] * 8 + x * 2 + cores[dc], y)))

    plane_me = x * 4 + y
    line_me = z * 2 + core
    arrival = y * 4 + x

    def fetch(at, source, target):
        copy = pltpu.make_async_copy(source, target, sems.at[at])
        copy.start()
        return copy

    fetch_x = fetch(0, table_x_ref.at[y], table_x)
    fetch_field = []
    for part in range(4):
        source = field_ref.at[part // 2, pl.ds(16 * (part % 2), 16)]
        fetch_field.append(fetch(1 + part, source, field.at[part // 2, pl.ds(16 * (part % 2), 16)]))
    fetch_y = fetch(5, table_y_ref, table_y)

    barrier = pltpu.get_barrier_semaphore()
    for _, device in line:
        pl.semaphore_signal(barrier, inc=1, device_id=device, device_id_type=MESH)
    for _, _, device in plane:
        pl.semaphore_signal(barrier, inc=1, device_id=device, device_id_type=MESH)

    fetch_owner = fetch(6, to_owner_ref, to_owner)
    fetch_center = [
        fetch(7, channels_ref, channels), fetch(8, table_z_ref, table_z), fetch(9, weight_ref, weight),
        fetch(10, turn_ref, turn), fetch(11, back_z_ref, back_z), fetch(12, to_grid_ref, to_grid),
        fetch(13, back_y_ref, back_y), fetch(14, back_x_ref.at[y], back_x),
    ]

    fetch_x.wait()
    for part in range(4):
        b, half = part // 2, part % 2
        fetch_field[part].wait()
        for inner in range(4):
            group = 4 * half + inner
            block = field[b, 4 * group : 4 * group + 4].reshape(256, NY)
            modes = jnp.dot(table_x[0], block, preferred_element_type=F32)
            modes += jnp.dot(table_x[1], block, preferred_element_type=F32)
            modes = modes.astype(BF16)
            for px in range(2):
                for hi in range(8):
                    row = (b * 8 + hi) * 128 + group * 16
                    at = (px * 8 + hi) * 16
                    along[row : row + 16, px * NY : (px + 1) * NY] = modes[at : at + 16]
    fetch_y.wait()
    for b in range(2):
        for half in range(2):
            row = (b * 2 + half) * 512
            pencil = lax.dot_general(
                table_y[...], along[row : row + 512], NT, preferred_element_type=F32
            ).astype(BF16)
            at = (b * 2 + half) * 16
            for xd in range(4):
                for yd in range(4):
                    send_a[xd * 4 + yd, at : at + 16, :] = pencil[
                        xd * 16 : xd * 16 + 16, yd * 128 : yd * 128 + 128
                    ]
    pl.semaphore_wait(barrier, 30)

    sent = []

    def send_plane(phase, source, target):
        for index, _, device in plane:
            copy = pltpu.make_async_remote_copy(
                src_ref=source(index), dst_ref=target.at[arrival],
                send_sem=send_sems.at[phase, index], recv_sem=recv_sems.at[phase, arrival],
                device_id=device, device_id_type=MESH,
            )
            copy.start()
            sent.append(copy)

    def send_line(phase, source, target):
        for index, device in line:
            copy = pltpu.make_async_remote_copy(
                src_ref=source.at[index], dst_ref=target.at[line_me],
                send_sem=send_sems.at[phase, index], recv_sem=recv_sems.at[phase, line_me],
                device_id=device, device_id_type=MESH,
            )
            copy.start()
            sent.append(copy)

    def arrived(phase, index, block):
        pltpu.make_async_copy(block, block, recv_sems.at[phase, index]).wait()

    send_plane(0, lambda index: send_a.at[index], got_a)
    got_a[arrival] = send_a[plane_me]

    row = lax.div(lax.broadcasted_iota(jnp.int32, (512, 32), 0), 16)
    lane = lax.broadcasted_iota(jnp.int32, (512, 32), 1)
    spread = (row == lane).astype(F32)
    bias = jnp.sum(spread * bias_ref[...], axis=1, keepdims=True)
    spread = spread.astype(BF16)
    wide = lax.dot_general(spread, bypass_ref[...], NT, preferred_element_type=F32).astype(BF16)
    wide = lax.dot_general(wide, spread, NT, preferred_element_type=F32)
    one = lax.rem(lax.broadcasted_iota(jnp.int32, (512, 512), 0), 16)
    two = lax.rem(lax.broadcasted_iota(jnp.int32, (512, 512), 1), 16)
    direct_table[...] = jnp.where(one == two, wide, 0.0).astype(BF16)

    def bypass(b):
        for group in range(4):
            block = field[b, :, group * 16 : group * 16 + 16, :].reshape(512, NY)
            values = bias + jnp.dot(direct_table[...], block, preferred_element_type=F32)
            direct[b, :, group * 16 : group * 16 + 16, :] = values.reshape(32, 16, NY)

    bypass(0)

    for _, slot, _ in plane:
        arrived(0, slot, got_a.at[slot])
    fetch_owner.wait()
    summed = jnp.zeros((256, 128), F32)
    for sy in range(4):
        summed += jnp.dot(
            to_owner[...], got_a[sy * 4 : sy * 4 + 4].reshape(256, 128), preferred_element_type=F32
        )
    send_b[...] = summed.astype(BF16).reshape(16, 16, 128)

    send_line(1, send_b, got_b)
    got_b[line_me] = send_b[line_me]
    bypass(1)
    for copy in fetch_center:
        copy.wait()

    for index, _ in line:
        arrived(1, index, got_b.at[index])
    pencils = lax.dot_general(
        channels[...], got_b[...].reshape(256, 128), NT, preferred_element_type=F32
    ).astype(BF16)
    rows = []
    for part in range(2):
        for j in range(4):
            rows.append([])
    for block in range(4):
        real_at, imag_at = block * 256, 1024 + block * 256
        real = jnp.dot(pencils, table_z[0, :, real_at : real_at + 256], preferred_element_type=F32)
        real += jnp.dot(pencils, table_z[1, :, real_at : real_at + 256], preferred_element_type=F32)
        imag = jnp.dot(pencils, table_z[0, :, imag_at : imag_at + 256], preferred_element_type=F32)
        imag += jnp.dot(pencils, table_z[1, :, imag_at : imag_at + 256], preferred_element_type=F32)
        for j in range(4):
            weight_real = weight[j, 0, :, real_at : real_at + 256].astype(F32)
            weight_imag = weight[j, 1, :, real_at : real_at + 256].astype(F32)
            one, two = real[j * 32 : j * 32 + 32], imag[j * 32 : j * 32 + 32]
            rows[j].append(jnp.sum(one * weight_real - two * weight_imag, axis=0, keepdims=True))
            rows[4 + j].append(jnp.sum(one * weight_imag + two * weight_real, axis=0, keepdims=True))
    mixed = jnp.concatenate([jnp.concatenate(row, axis=1) for row in rows], axis=0)
    mixed = jnp.concatenate([mixed[:, h * 128 : h * 128 + 128] for h in range(8)], axis=0)
    turned = jnp.dot(mixed.astype(BF16), turn[...], preferred_element_type=F32)
    turned = jnp.concatenate([turned[:, t * 128 : t * 128 + 128] for t in range(4)], axis=0)
    row = lax.broadcasted_iota(jnp.int32, (256, 128), 0)
    lane = lax.broadcasted_iota(jnp.int32, (256, 128), 1)
    turned = jnp.where(lax.rem(row, 4) == lax.rem(lax.div(lane, 4), 4), turned, 0.0).astype(BF16)
    planes = jnp.dot(back_z[0], turned, preferred_element_type=F32)
    planes += jnp.dot(back_z[1], turned, preferred_element_type=F32)
    back_b[...] = planes.astype(BF16).reshape(16, 16, 128)

    send_line(2, back_b, home_b)
    home_b[line_me] = back_b[line_me]

    for index, _ in line:
        arrived(2, index, home_b.at[index])
    home = jnp.dot(to_grid[...], home_b[...].reshape(256, 128), preferred_element_type=F32)
    back_a[...] = home.astype(BF16).reshape(4, 64, 128)

    send_plane(3, lambda index: back_a.at[lax.shift_right_logical(index, 2)], home_a)
    home_a[arrival] = back_a[x]

    for dy in (0, 1, 3, 2):
        for dx in range(4):
            if dx or dy:
                slot = ys[dy] * 4 + xs[dx]
                arrived(3, slot, home_a.at[slot])
        rows = jnp.concatenate(
            [home_a[pl.ds(ys[dy] * 4, 4), at : at + 16, :].reshape(64, 128) for at in range(0, 64, 16)], axis=1
        )
        rows = jnp.concatenate([rows, rows], axis=0)
        values = lax.dot_general(rows, back_y[...], TN, preferred_element_type=F32).astype(BF16)
        for b in range(2):
            for half in range(2):
                for part in range(2):
                    at = pl.multiple_of((part * 8 + half * 4 + ys[dy]) * 16, 16)
                    for group in range(8):
                        row = (b * 2 + half) * 128 + group * 16
                        lines[b, group, pl.ds(at, 16), :] = values[
                            row : row + 16, part * NY : (part + 1) * NY
                        ]

    def store(b, group):
        rows = pl.ds(group * 4, 4)
        return pltpu.make_async_copy(result.at[b, rows], out_ref.at[b, rows], store_sems.at[b, group])

    def finish(group, carry):
        for b in range(2):
            values = jnp.dot(back_x[...], lines[b, group], preferred_element_type=F32)
            rows = pl.ds(group * 4, 4)
            total = values[:256] + values[256:] + direct[b, rows].reshape(256, NY)
            total = 0.5 * total * (1.0 + lax.erf(total * (1.0 / math.sqrt(2.0))))
            result[b, rows] = total.astype(BF16).reshape(4, 64, NY)
            store(b, group).start()
        return carry

    lax.fori_loop(0, 8, finish, 0)
    for copy in sent:
        copy.wait_send()

    def stored(group, carry):
        for b in range(2):
            store(b, group).wait()
        return carry

    lax.fori_loop(0, 8, stored, 0)


VMEM = pl.BlockSpec(memory_space=pltpu.VMEM)
HBM = pl.BlockSpec(memory_space=pltpu.HBM)


def shards(field, spectral_weight, bypass_weight, bypass_bias):
    return pl.pallas_call(
        exchange_kernel,
        out_shape=jax.ShapeDtypeStruct(field.shape, BF16),
        in_specs=[HBM] * 12 + [VMEM] * 2,
        out_specs=HBM,
        scratch_shapes=[
            pltpu.VMEM((16, 64, 128), BF16),
            pltpu.VMEM((16, 64, 128), BF16),
            pltpu.VMEM((16, 16, 128), BF16),
            pltpu.VMEM((16, 16, 128), BF16),
            pltpu.VMEM((16, 16, 128), BF16),
            pltpu.VMEM((16, 16, 128), BF16),
            pltpu.VMEM((4, 64, 128), BF16),
            pltpu.VMEM((16, 64, 128), BF16),
            pltpu.VMEM((2, 32, 64, NY), BF16),
            pltpu.VMEM((2, 256, 256), BF16),
            pltpu.VMEM((64, 2 * NY), BF16),
            pltpu.VMEM((2048, 2 * NY), BF16),
            pltpu.VMEM((4, 2, 32, 1024), BF16),
            pltpu.VMEM((256, 256), BF16),
            pltpu.VMEM((128, 128), BF16),
            pltpu.VMEM((2, 256, 2048), BF16),
            pltpu.VMEM((128, 512), BF16),
            pltpu.VMEM((2, 256, 256), BF16),
            pltpu.VMEM((256, 256), BF16),
            pltpu.VMEM((128, 512), BF16),
            pltpu.VMEM((512, 256), BF16),
            pltpu.VMEM((512, 512), BF16),
            pltpu.VMEM((2, 32, 64, NY), F32),
            pltpu.VMEM((2, 8, 256, NY), BF16),
            pltpu.VMEM((2, 32, 64, NY), BF16),
            pltpu.SemaphoreType.DMA((15,)),
            pltpu.SemaphoreType.DMA((4, 16)),
            pltpu.SemaphoreType.DMA((4, 16)),
            pltpu.SemaphoreType.DMA((2, 8)),
        ],
        compiler_params=pltpu.CompilerParams(
            collective_id=0, has_side_effects=True, vmem_limit_bytes=60 << 20
        ),
        name="exchange",
    )(
        field, jnp.asarray(forward_x()), jnp.asarray(forward_y()),
        spectral_weight, jnp.asarray(order_to_owner()), jnp.asarray(order_channels()),
        jnp.asarray(forward_z()), jnp.asarray(turn_lanes()), jnp.asarray(inverse_z()),
        jnp.asarray(order_to_grid()), jnp.asarray(inverse_y()), jnp.asarray(inverse_x()),
        bypass_weight, bypass_bias.reshape(1, 32),
    )


def solution(mesh):
    in_specs = (P("gz", None, "gx", None), P(("gz", "gx"), None, None, None), P(), P())
    out_specs = P("gz", None, "gx", None)
    return jax.shard_map(shards, mesh=mesh, in_specs=in_specs, out_specs=out_specs, check_vma=False)
```

```python
import math

import jax
import jax.numpy as jnp
import ml_dtypes
import numpy as np
from jax import lax
from jax.experimental import pallas as pl
from jax.experimental.pallas import tpu as pltpu
from jax.sharding import PartitionSpec as P

NX, NY, NZ = 256, 256, 128
BF16 = jnp.bfloat16
F32 = jnp.float32
MESH = pl.DeviceIdType.MESH
NT = (((1,), (1,)), ((), ()))
TN = (((0,), (0,)), ((), ()))


def ring(step, size):
    return min(step, size - step)


PLANE = sorted(
    [(dx, dy) for dx in range(4) for dy in range(4) if dx or dy], key=lambda step: -ring(step[0], 4) - ring(step[1], 4)
)
LINE = sorted(
    [(dz, dc) for dz in range(8) for dc in range(2) if dz or dc], key=lambda step: -ring(step[0], 8) - 0.1 * step[1]
)


def split(table):
    high = table.astype(ml_dtypes.bfloat16)
    low = (table - high.astype(np.float64)).astype(ml_dtypes.bfloat16)
    return high, low


def wave(frequency, place, length):
    angle = 2.0 * math.pi * np.mod(frequency * place, length) / length
    return np.cos(angle), np.sin(angle)


def signed(mode):
    return np.where(mode < 16, mode, mode - 32)


def axes(*sizes):
    return np.meshgrid(*[np.arange(size) for size in sizes], indexing="ij")


def one_hot(rows, columns, size):
    table = np.zeros((size, size), np.float64)
    table[rows.reshape(-1), columns.reshape(-1)] = 1.0
    return table.astype(ml_dtypes.bfloat16)


def forward_x():
    gx, px, hi, j, c, cc, x = axes(4, 2, 8, 4, 4, 4, 64)
    cos, sin = wave(signed(4 * hi + j), 64 * gx + x, NX)
    table = np.where(px == 0, cos, -sin) * (c == cc)
    return np.stack(split(table.reshape(4, 256, 256)), axis=1)


def forward_y():
    xd, part, zd, px, y = axes(4, 2, 8, 2, NY)
    cos, sin = wave(signed(4 * zd + xd), y, NY)
    table = np.where(px == part, cos, np.where(part == 0, sin, -sin))
    return table.reshape(64, 2 * NY).astype(ml_dtypes.bfloat16)


def order_to_owner():
    xs, b, core, part, zd = axes(4, 2, 2, 2, 8)
    source = (((xs * 2 + b) * 2 + core) * 2 + part) * 8 + zd
    target = (((zd * 2 + core) * 4 + xs) * 2 + b) * 2 + part
    return one_hot(target, source, 256)


def order_to_grid():
    xs, b, core, part, zs = axes(4, 2, 2, 2, 8)
    target = (((xs * 2 + b) * 2 + core) * 2 + part) * 8 + zs
    source = (((zs * 2 + core) * 4 + xs) * 2 + b) * 2 + part
    return one_hot(target, source, 256)


def order_channels():
    j, i = axes(4, 32)
    return one_hot(j * 32 + i, (i // 4) * 16 + j * 4 + i % 4, 128)


def forward_z():
    zs, core, xs, b, part, part_out, kz, o = axes(8, 2, 4, 2, 2, 2, 32, 32)
    cos, sin = wave(kz, 16 * zs + 4 * xs + 2 * core + b, NZ)
    table = np.where(part == part_out, cos, np.where(part_out == 0, sin, -sin)) / math.sqrt(NX * NY * NZ)
    return np.stack(split(table.reshape(256, 2048)))


def turn_lanes():
    table = np.zeros((128, 4, 128), np.float64)
    turn, low, o = axes(4, 4, 32)
    j = (low + turn) % 4
    table[low * 32 + o, turn, (o // 4) * 16 + j * 4 + o % 4] = 1.0
    return table.reshape(128, 512).astype(ml_dtypes.bfloat16)


def inverse_z():
    zd, core, xd, b, part_out, turn, high, part, j = axes(8, 2, 4, 2, 2, 4, 8, 2, 4)
    kz = 4 * high + (j - turn) % 4
    cos, sin = wave(kz, 16 * zd + 4 * xd + 2 * core + b, NZ)
    table = np.where(part == part_out, cos, np.where(part_out == 0, -sin, sin))
    table = table * np.where(kz == 0, 1.0, 2.0) / (2.0 * math.sqrt(32 * 32 * 32))
    return np.stack(split(table.reshape(256, 256)))


def inverse_y():
    xs, part, zs, part_out, y = axes(4, 2, 8, 2, NY)
    cos, sin = wave(signed(4 * zs + xs), y, NY)
    table = np.where(part == part_out, cos, np.where(part_out == 0, -sin, sin))
    return np.concatenate(split(table.reshape(64, 2 * NY)))


def inverse_x():
    gx, o, x, part, hi, j, oo = axes(4, 4, 64, 2, 8, 4, 4)
    cos, sin = wave(signed(4 * hi + j), 64 * gx + x, NX)
    table = np.where(part == 0, cos, -sin) * (o == oo)
    return np.concatenate(split(table.reshape(4, 256, 256)), axis=1)


def exchange_kernel(
    field_ref, table_x_ref, table_y_ref, weight_ref, to_owner_ref, channels_ref, table_z_ref, turn_ref,
    back_z_ref, to_grid_ref, back_y_ref, back_x_ref, bypass_ref, bias_ref,
    out_ref,
    send_a, got_a, send_b, got_b, back_b, home_b, back_a, home_a,
    field, table_x, table_y, along, weight, to_owner, channels, table_z, turn, back_z, to_grid,
    back_y, back_x, direct_table, direct, lines, result,
    sems, send_sems, recv_sems, store_sems,
):
    gz = lax.axis_index("gz")
    y = lax.axis_index("gx")
    core = gz & 1
    x = lax.shift_right_logical(gz, 1) & 3
    z = lax.shift_right_logical(gz, 3)
    xs = [(x + step) & 3 for step in range(4)]
    ys = [(y + step) & 3 for step in range(4)]
    zs = [(z + step) & 7 for step in range(8)]
    cores = [core, 1 - core]

    plane = []
    for dx, dy in PLANE:
        plane.append((xs[dx] * 4 + ys[dy], ys[dy] * 4 + xs[dx], (z * 8 + xs[dx] * 2 + core, ys[dy])))
    line = []
    for dz, dc in LINE:
        line.append((zs[dz] * 2 + cores[dc], (zs[dz] * 8 + x * 2 + cores[dc], y)))

    plane_me = x * 4 + y
    line_me = z * 2 + core
    arrival = y * 4 + x

    barrier = pltpu.get_barrier_semaphore()
    for near in range(4, -1, -1):
        for (dz, _), (_, device) in zip(LINE, line):
            if ring(dz, 8) == near:
                pl.semaphore_signal(barrier, inc=1, device_id=device, device_id_type=MESH)
        for (dx, dy), (_, _, device) in zip(PLANE, plane):
            if ring(dx, 4) + ring(dy, 4) == near:
                pl.semaphore_signal(barrier, inc=1, device_id=device, device_id_type=MESH)

    def fetch(at, source, target):
        copy = pltpu.make_async_copy(source, target, sems.at[at])
        copy.start()
        return copy

    fetch_x = fetch(0, table_x_ref.at[y], table_x)
    fetch_field = []
    for part in range(4):
        source = field_ref.at[part // 2, pl.ds(16 * (part % 2), 16)]
        fetch_field.append(fetch(1 + part, source, field.at[part // 2, pl.ds(16 * (part % 2), 16)]))
    fetch_y = fetch(5, table_y_ref, table_y)

    fetch_owner = fetch(6, to_owner_ref, to_owner)
    fetch_center = [
        fetch(7, channels_ref, channels), fetch(8, table_z_ref, table_z), fetch(9, weight_ref, weight),
        fetch(10, turn_ref, turn), fetch(11, back_z_ref, back_z), fetch(12, to_grid_ref, to_grid),
        fetch(13, back_y_ref, back_y), fetch(14, back_x_ref.at[y], back_x),
    ]

    fetch_x.wait()
    for part in range(4):
        b, half = part // 2, part % 2
        fetch_field[part].wait()
        for inner in range(4):
            group = 4 * half + inner
            block = field[b, 4 * group : 4 * group + 4].reshape(256, NY)
            modes = jnp.dot(table_x[0], block, preferred_element_type=F32)
            modes += jnp.dot(table_x[1], block, preferred_element_type=F32)
            modes = modes.astype(BF16)
            for px in range(2):
                for hi in range(8):
                    row = (b * 8 + hi) * 128 + group * 16
                    at = (px * 8 + hi) * 16
                    along[row : row + 16, px * NY : (px + 1) * NY] = modes[at : at + 16]
    fetch_y.wait()
    for b in range(2):
        for half in range(2):
            row = (b * 2 + half) * 512
            pencil = lax.dot_general(
                table_y[...], along[row : row + 512], NT, preferred_element_type=F32
            ).astype(BF16)
            at = (b * 2 + half) * 16
            for xd in range(4):
                for yd in range(4):
                    send_a[xd * 4 + yd, at : at + 16, :] = pencil[
                        xd * 16 : xd * 16 + 16, yd * 128 : yd * 128 + 128
                    ]
    pl.semaphore_wait(barrier, 30)

    sent = []

    def send_plane(phase, source, target):
        for index, _, device in plane:
            copy = pltpu.make_async_remote_copy(
                src_ref=source(index), dst_ref=target.at[arrival],
                send_sem=send_sems.at[phase, index], recv_sem=recv_sems.at[phase, arrival],
                device_id=device, device_id_type=MESH,
            )
            copy.start()
            sent.append(copy)

    def send_line(phase, source, target):
        for index, device in line:
            copy = pltpu.make_async_remote_copy(
                src_ref=source.at[index], dst_ref=target.at[line_me],
                send_sem=send_sems.at[phase, index], recv_sem=recv_sems.at[phase, line_me],
                device_id=device, device_id_type=MESH,
            )
            copy.start()
            sent.append(copy)

    def arrived(phase, index, block):
        pltpu.make_async_copy(block, block, recv_sems.at[phase, index]).wait()

    send_plane(0, lambda index: send_a.at[index], got_a)
    got_a[arrival] = send_a[plane_me]

    row = lax.div(lax.broadcasted_iota(jnp.int32, (512, 32), 0), 16)
    lane = lax.broadcasted_iota(jnp.int32, (512, 32), 1)
    spread = (row == lane).astype(F32)
    bias = jnp.sum(spread * bias_ref[...], axis=1, keepdims=True)
    spread = spread.astype(BF16)
    wide = lax.dot_general(spread, bypass_ref[...], NT, preferred_element_type=F32).astype(BF16)
    wide = lax.dot_general(wide, spread, NT, preferred_element_type=F32)
    one = lax.rem(lax.broadcasted_iota(jnp.int32, (512, 512), 0), 16)
    two = lax.rem(lax.broadcasted_iota(jnp.int32, (512, 512), 1), 16)
    direct_table[...] = jnp.where(one == two, wide, 0.0).astype(BF16)

    def bypass(b):
        for group in range(4):
            block = field[b, :, group * 16 : group * 16 + 16, :].reshape(512, NY)
            values = bias + jnp.dot(direct_table[...], block, preferred_element_type=F32)
            direct[b, :, group * 16 : group * 16 + 16, :] = values.reshape(32, 16, NY)

    bypass(0)

    for _, slot, _ in plane:
        arrived(0, slot, got_a.at[slot])
    fetch_owner.wait()
    summed = jnp.zeros((256, 128), F32)
    for sy in range(4):
        summed += jnp.dot(
            to_owner[...], got_a[sy * 4 : sy * 4 + 4].reshape(256, 128), preferred_element_type=F32
        )
    send_b[...] = summed.astype(BF16).reshape(16, 16, 128)

    send_line(1, send_b, got_b)
    got_b[line_me] = send_b[line_me]
    bypass(1)
    for copy in fetch_center:
        copy.wait()

    for index, _ in line:
        arrived(1, index, got_b.at[index])
    pencils = lax.dot_general(
        channels[...], got_b[...].reshape(256, 128), NT, preferred_element_type=F32
    ).astype(BF16)
    rows = []
    for part in range(2):
        for j in range(4):
            rows.append([])
    for block in range(4):
        real_at, imag_at = block * 256, 1024 + block * 256
        real = jnp.dot(pencils, table_z[0, :, real_at : real_at + 256], preferred_element_type=F32)
        real += jnp.dot(pencils, table_z[1, :, real_at : real_at + 256], preferred_element_type=F32)
        imag = jnp.dot(pencils, table_z[0, :, imag_at : imag_at + 256], preferred_element_type=F32)
        imag += jnp.dot(pencils, table_z[1, :, imag_at : imag_at + 256], preferred_element_type=F32)
        for j in range(4):
            weight_real = weight[j, 0, :, real_at : real_at + 256].astype(F32)
            weight_imag = weight[j, 1, :, real_at : real_at + 256].astype(F32)
            one, two = real[j * 32 : j * 32 + 32], imag[j * 32 : j * 32 + 32]
            rows[j].append(jnp.sum(one * weight_real - two * weight_imag, axis=0, keepdims=True))
            rows[4 + j].append(jnp.sum(one * weight_imag + two * weight_real, axis=0, keepdims=True))
    mixed = jnp.concatenate([jnp.concatenate(row, axis=1) for row in rows], axis=0)
    mixed = jnp.concatenate([mixed[:, h * 128 : h * 128 + 128] for h in range(8)], axis=0)
    turned = jnp.dot(mixed.astype(BF16), turn[...], preferred_element_type=F32)
    turned = jnp.concatenate([turned[:, t * 128 : t * 128 + 128] for t in range(4)], axis=0)
    row = lax.broadcasted_iota(jnp.int32, (256, 128), 0)
    lane = lax.broadcasted_iota(jnp.int32, (256, 128), 1)
    turned = jnp.where(lax.rem(row, 4) == lax.rem(lax.div(lane, 4), 4), turned, 0.0).astype(BF16)
    planes = jnp.dot(back_z[0], turned, preferred_element_type=F32)
    planes += jnp.dot(back_z[1], turned, preferred_element_type=F32)
    back_b[...] = planes.astype(BF16).reshape(16, 16, 128)

    send_line(2, back_b, home_b)
    home_b[line_me] = back_b[line_me]

    for index, _ in line:
        arrived(2, index, home_b.at[index])
    home = jnp.dot(to_grid[...], home_b[...].reshape(256, 128), preferred_element_type=F32)
    back_a[...] = home.astype(BF16).reshape(4, 64, 128)

    send_plane(3, lambda index: back_a.at[lax.shift_right_logical(index, 2)], home_a)
    home_a[arrival] = back_a[x]

    def store(b, group):
        rows = pl.ds(group * 4, 4)
        return pltpu.make_async_copy(result.at[b, rows], out_ref.at[b, rows], store_sems.at[b, group])

    for b in range(2):
        for dy in (0, 1, 3, 2):
            for dx in range(4):
                if b == 0 and (dx or dy):
                    slot = ys[dy] * 4 + xs[dx]
                    arrived(3, slot, home_a.at[slot])
            rows = jnp.concatenate(
                [
                    home_a[pl.ds(ys[dy] * 4, 4), at : at + 16, :].reshape(64, 128)
                    for at in (b * 32, b * 32 + 16)
                ],
                axis=1,
            )
            rows = jnp.concatenate([rows, rows], axis=0)
            values = lax.dot_general(rows, back_y[...], TN, preferred_element_type=F32).astype(BF16)
            for half in range(2):
                for part in range(2):
                    at = pl.multiple_of((part * 8 + half * 4 + ys[dy]) * 16, 16)
                    for group in range(8):
                        row = half * 128 + group * 16
                        lines[b, group, pl.ds(at, 16), :] = values[
                            row : row + 16, part * NY : (part + 1) * NY
                        ]
        for group in range(8):
            values = jnp.dot(back_x[...], lines[b, group], preferred_element_type=F32)
            channels = slice(group * 4, group * 4 + 4)
            total = values[:256] + values[256:] + direct[b, channels].reshape(256, NY)
            total = 0.5 * total * (1.0 + lax.erf(total * (1.0 / math.sqrt(2.0))))
            result[b, channels] = total.astype(BF16).reshape(4, 64, NY)
            store(b, group).start()
    for copy in sent:
        copy.wait_send()

    def stored(group, carry):
        for b in range(2):
            store(b, group).wait()
        return carry

    lax.fori_loop(0, 8, stored, 0)


def hand_over_kernel(source_ref, out_ref, held, load_sems, store_sems):
    def load(part):
        at = (part // 4, pl.ds(part % 4 * 8, 8))
        return pltpu.make_async_copy(source_ref.at[at], held.at[at], load_sems.at[part])

    def store(part):
        at = (part // 4, pl.ds(part % 4 * 8, 8))
        return pltpu.make_async_copy(held.at[at], out_ref.at[at], store_sems.at[part])

    for part in range(8):
        load(part).start()
    for part in range(8):
        load(part).wait()
        store(part).start()
    for part in range(8):
        store(part).wait()


VMEM = pl.BlockSpec(memory_space=pltpu.VMEM)
HBM = pl.BlockSpec(memory_space=pltpu.HBM)


def shards(field, spectral_weight, bypass_weight, bypass_bias):
    result = pl.pallas_call(
        exchange_kernel,
        out_shape=jax.ShapeDtypeStruct(field.shape, BF16),
        in_specs=[HBM] * 12 + [VMEM] * 2,
        out_specs=HBM,
        scratch_shapes=[
            pltpu.VMEM((16, 64, 128), BF16),
            pltpu.VMEM((16, 64, 128), BF16),
            pltpu.VMEM((16, 16, 128), BF16),
            pltpu.VMEM((16, 16, 128), BF16),
            pltpu.VMEM((16, 16, 128), BF16),
            pltpu.VMEM((16, 16, 128), BF16),
            pltpu.VMEM((4, 64, 128), BF16),
            pltpu.VMEM((16, 64, 128), BF16),
            pltpu.VMEM((2, 32, 64, NY), BF16),
            pltpu.VMEM((2, 256, 256), BF16),
            pltpu.VMEM((64, 2 * NY), BF16),
            pltpu.VMEM((2048, 2 * NY), BF16),
            pltpu.VMEM((4, 2, 32, 1024), BF16),
            pltpu.VMEM((256, 256), BF16),
            pltpu.VMEM((128, 128), BF16),
            pltpu.VMEM((2, 256, 2048), BF16),
            pltpu.VMEM((128, 512), BF16),
            pltpu.VMEM((2, 256, 256), BF16),
            pltpu.VMEM((256, 256), BF16),
            pltpu.VMEM((128, 512), BF16),
            pltpu.VMEM((512, 256), BF16),
            pltpu.VMEM((512, 512), BF16),
            pltpu.VMEM((2, 32, 64, NY), F32),
            pltpu.VMEM((2, 8, 256, NY), BF16),
            pltpu.VMEM((2, 32, 64, NY), BF16),
            pltpu.SemaphoreType.DMA((15,)),
            pltpu.SemaphoreType.DMA((4, 16)),
            pltpu.SemaphoreType.DMA((4, 16)),
            pltpu.SemaphoreType.DMA((2, 8)),
        ],
        compiler_params=pltpu.CompilerParams(
            collective_id=0, has_side_effects=True, vmem_limit_bytes=60 << 20
        ),
        name="exchange",
    )(
        field, jnp.asarray(forward_x()), jnp.asarray(forward_y()),
        spectral_weight, jnp.asarray(order_to_owner()), jnp.asarray(order_channels()),
        jnp.asarray(forward_z()), jnp.asarray(turn_lanes()), jnp.asarray(inverse_z()),
        jnp.asarray(order_to_grid()), jnp.asarray(inverse_y()), jnp.asarray(inverse_x()),
        bypass_weight, bypass_bias.reshape(1, 32),
    )

    return pl.pallas_call(
        hand_over_kernel,
        out_shape=jax.ShapeDtypeStruct(field.shape, BF16),
        in_specs=[HBM],
        out_specs=HBM,
        scratch_shapes=[
            pltpu.VMEM((2, 32, 64, NY), BF16),
            pltpu.SemaphoreType.DMA((8,)),
            pltpu.SemaphoreType.DMA((8,)),
        ],
        compiler_params=pltpu.CompilerParams(vmem_limit_bytes=60 << 20),
        name="hand_over",
    )(result)


def solution(mesh):
    in_specs = (P("gz", None, "gx", None), P(("gz", "gx"), None, None, None), P(), P())
    out_specs = P("gz", None, "gx", None)
    return jax.shard_map(shards, mesh=mesh, in_specs=in_specs, out_specs=out_specs, check_vma=False)
```

```python
import math

import jax
import jax.numpy as jnp
import ml_dtypes
import numpy as np
from jax import lax
from jax.experimental import pallas as pl
from jax.experimental.pallas import tpu as pltpu
from jax.sharding import PartitionSpec as P

NX, NY, NZ = 256, 256, 128
BF16 = jnp.bfloat16
F32 = jnp.float32
MESH = pl.DeviceIdType.MESH
NT = (((1,), (1,)), ((), ()))
TN = (((0,), (0,)), ((), ()))


def ring(step, size):
    return min(step, size - step)


PLANE = sorted(
    [(dx, dy) for dx in range(4) for dy in range(4) if dx or dy], key=lambda step: -ring(step[0], 4) - ring(step[1], 4)
)
LINE = sorted(
    [(dz, dc) for dz in range(8) for dc in range(2) if dz or dc], key=lambda step: -ring(step[0], 8) - 0.1 * step[1]
)


def split(table):
    high = table.astype(ml_dtypes.bfloat16)
    low = (table - high.astype(np.float64)).astype(ml_dtypes.bfloat16)
    return high, low


def wave(frequency, place, length):
    angle = 2.0 * math.pi * np.mod(frequency * place, length) / length
    return np.cos(angle), np.sin(angle)


def signed(mode):
    return np.where(mode < 16, mode, mode - 32)


def axes(*sizes):
    return np.meshgrid(*[np.arange(size) for size in sizes], indexing="ij")


def one_hot(rows, columns, size):
    table = np.zeros((size, size), np.float64)
    table[rows.reshape(-1), columns.reshape(-1)] = 1.0
    return table.astype(ml_dtypes.bfloat16)


def forward_x():
    gx, px, hi, j, c, cc, x = axes(4, 2, 8, 4, 4, 4, 64)
    cos, sin = wave(signed(4 * hi + j), 64 * gx + x, NX)
    table = np.where(px == 0, cos, -sin) * (c == cc)
    return np.stack(split(table.reshape(4, 256, 256)), axis=1)


def forward_y():
    xd, part, zd, px, y = axes(4, 2, 8, 2, NY)
    cos, sin = wave(signed(4 * zd + xd), y, NY)
    table = np.where(px == part, cos, np.where(part == 0, sin, -sin))
    return table.reshape(64, 2 * NY).astype(ml_dtypes.bfloat16)


def order_to_owner():
    xs, b, core, part, zd = axes(4, 2, 2, 2, 8)
    source = (((xs * 2 + b) * 2 + core) * 2 + part) * 8 + zd
    target = (((zd * 2 + core) * 4 + xs) * 2 + b) * 2 + part
    return one_hot(target, source, 256)


def order_to_grid():
    xs, b, core, part, zs = axes(4, 2, 2, 2, 8)
    target = (((xs * 2 + b) * 2 + core) * 2 + part) * 8 + zs
    source = (((zs * 2 + core) * 4 + xs) * 2 + b) * 2 + part
    return one_hot(target, source, 256)


def order_channels():
    j, i = axes(4, 32)
    return one_hot(j * 32 + i, (i // 4) * 16 + j * 4 + i % 4, 128)


def forward_z():
    zs, core, xs, b, part, part_out, kz, o = axes(8, 2, 4, 2, 2, 2, 32, 32)
    cos, sin = wave(kz, 16 * zs + 4 * xs + 2 * core + b, NZ)
    table = np.where(part == part_out, cos, np.where(part_out == 0, sin, -sin)) / math.sqrt(NX * NY * NZ)
    return np.stack(split(table.reshape(256, 2048)))


def turn_lanes():
    table = np.zeros((128, 4, 128), np.float64)
    turn, low, o = axes(4, 4, 32)
    j = (low + turn) % 4
    table[low * 32 + o, turn, (o // 4) * 16 + j * 4 + o % 4] = 1.0
    return table.reshape(128, 512).astype(ml_dtypes.bfloat16)


def inverse_z():
    zd, core, xd, b, part_out, turn, high, part, j = axes(8, 2, 4, 2, 2, 4, 8, 2, 4)
    kz = 4 * high + (j - turn) % 4
    cos, sin = wave(kz, 16 * zd + 4 * xd + 2 * core + b, NZ)
    table = np.where(part == part_out, cos, np.where(part_out == 0, -sin, sin))
    table = table * np.where(kz == 0, 1.0, 2.0) / (2.0 * math.sqrt(32 * 32 * 32))
    return np.stack(split(table.reshape(256, 256)))


def inverse_y():
    xs, part, zs, part_out, y = axes(4, 2, 8, 2, NY)
    cos, sin = wave(signed(4 * zs + xs), y, NY)
    table = np.where(part == part_out, cos, np.where(part_out == 0, -sin, sin))
    return np.concatenate(split(table.reshape(64, 2 * NY)))


def inverse_x():
    gx, o, x, part, hi, j, oo = axes(4, 4, 64, 2, 8, 4, 4)
    cos, sin = wave(signed(4 * hi + j), 64 * gx + x, NX)
    table = np.where(part == 0, cos, -sin) * (o == oo)
    return np.concatenate(split(table.reshape(4, 256, 256)), axis=1)


def exchange_kernel(
    field_ref, table_x_ref, table_y_ref, weight_ref, to_owner_ref, channels_ref, table_z_ref, turn_ref,
    back_z_ref, to_grid_ref, back_y_ref, back_x_ref, bypass_ref, bias_ref,
    out_ref,
    send_a, got_a, send_b, got_b, back_b, home_b, back_a, home_a,
    field, table_x, table_y, along, weight, to_owner, channels, table_z, turn, back_z, to_grid,
    back_y, back_x, direct_table, direct, lines_first, lines_second, result,
    sems, send_sems, recv_sems, store_sems,
):
    gz = lax.axis_index("gz")
    y = lax.axis_index("gx")
    core = gz & 1
    x = lax.shift_right_logical(gz, 1) & 3
    z = lax.shift_right_logical(gz, 3)
    xs = [(x + step) & 3 for step in range(4)]
    ys = [(y + step) & 3 for step in range(4)]
    zs = [(z + step) & 7 for step in range(8)]
    cores = [core, 1 - core]

    plane = []
    for dx, dy in PLANE:
        plane.append((xs[dx] * 4 + ys[dy], ys[dy] * 4 + xs[dx], (z * 8 + xs[dx] * 2 + core, ys[dy])))
    line = []
    for dz, dc in LINE:
        line.append((zs[dz] * 2 + cores[dc], (zs[dz] * 8 + x * 2 + cores[dc], y)))

    plane_me = x * 4 + y
    line_me = z * 2 + core
    arrival = y * 4 + x

    barrier = pltpu.get_barrier_semaphore()
    for near in range(4, -1, -1):
        for (dz, _), (_, device) in zip(LINE, line):
            if ring(dz, 8) == near:
                pl.semaphore_signal(barrier, inc=1, device_id=device, device_id_type=MESH)
        for (dx, dy), (_, _, device) in zip(PLANE, plane):
            if ring(dx, 4) + ring(dy, 4) == near:
                pl.semaphore_signal(barrier, inc=1, device_id=device, device_id_type=MESH)

    def fetch(at, source, target):
        copy = pltpu.make_async_copy(source, target, sems.at[at])
        copy.start()
        return copy

    fetch_x = fetch(0, table_x_ref.at[y], table_x)
    fetch_field = []
    for part in range(4):
        source = field_ref.at[part // 2, pl.ds(16 * (part % 2), 16)]
        fetch_field.append(fetch(1 + part, source, field.at[part // 2, pl.ds(16 * (part % 2), 16)]))
    fetch_y = fetch(5, table_y_ref, table_y)

    fetch_owner = fetch(6, to_owner_ref, to_owner)
    fetch_center = [
        fetch(7, channels_ref, channels), fetch(8, table_z_ref, table_z), fetch(9, weight_ref, weight),
        fetch(10, turn_ref, turn), fetch(11, back_z_ref, back_z), fetch(12, to_grid_ref, to_grid),
        fetch(13, back_y_ref, back_y), fetch(14, back_x_ref.at[y], back_x),
    ]

    fetch_x.wait()
    for part in range(4):
        b, half = part // 2, part % 2
        fetch_field[part].wait()
        for inner in range(4):
            group = 4 * half + inner
            block = field[b, 4 * group : 4 * group + 4].reshape(256, NY)
            modes = jnp.dot(table_x[0], block, preferred_element_type=F32)
            modes += jnp.dot(table_x[1], block, preferred_element_type=F32)
            modes = modes.astype(BF16)
            for px in range(2):
                for hi in range(8):
                    row = (b * 8 + hi) * 128 + group * 16
                    at = (px * 8 + hi) * 16
                    along[row : row + 16, px * NY : (px + 1) * NY] = modes[at : at + 16]
    fetch_y.wait()
    for b in range(2):
        for half in range(2):
            row = (b * 2 + half) * 512
            pencil = lax.dot_general(
                table_y[...], along[row : row + 512], NT, preferred_element_type=F32
            ).astype(BF16)
            at = (b * 2 + half) * 16
            for xd in range(4):
                for yd in range(4):
                    send_a[xd * 4 + yd, at : at + 16, :] = pencil[
                        xd * 16 : xd * 16 + 16, yd * 128 : yd * 128 + 128
                    ]
    pl.semaphore_wait(barrier, 30)

    sent = []

    def send_plane(phase, source, target):
        for index, _, device in plane:
            copy = pltpu.make_async_remote_copy(
                src_ref=source(index), dst_ref=target.at[arrival],
                send_sem=send_sems.at[phase, index], recv_sem=recv_sems.at[phase, arrival],
                device_id=device, device_id_type=MESH,
            )
            copy.start()
            sent.append(copy)

    def send_line(phase, source, target):
        for index, device in line:
            copy = pltpu.make_async_remote_copy(
                src_ref=source.at[index], dst_ref=target.at[line_me],
                send_sem=send_sems.at[phase, index], recv_sem=recv_sems.at[phase, line_me],
                device_id=device, device_id_type=MESH,
            )
            copy.start()
            sent.append(copy)

    def arrived(phase, index, block):
        pltpu.make_async_copy(block, block, recv_sems.at[phase, index]).wait()

    send_plane(0, lambda index: send_a.at[index], got_a)
    got_a[arrival] = send_a[plane_me]

    row = lax.div(lax.broadcasted_iota(jnp.int32, (512, 32), 0), 16)
    lane = lax.broadcasted_iota(jnp.int32, (512, 32), 1)
    spread = (row == lane).astype(F32)
    bias = jnp.sum(spread * bias_ref[...], axis=1, keepdims=True)
    spread = spread.astype(BF16)
    wide = lax.dot_general(spread, bypass_ref[...], NT, preferred_element_type=F32).astype(BF16)
    wide = lax.dot_general(wide, spread, NT, preferred_element_type=F32)
    one = lax.rem(lax.broadcasted_iota(jnp.int32, (512, 512), 0), 16)
    two = lax.rem(lax.broadcasted_iota(jnp.int32, (512, 512), 1), 16)
    direct_table[...] = jnp.where(one == two, wide, 0.0).astype(BF16)

    def bypass(b):
        for group in range(4):
            block = field[b, :, group * 16 : group * 16 + 16, :].reshape(512, NY)
            values = bias + jnp.dot(direct_table[...], block, preferred_element_type=F32)
            direct[b, :, group * 16 : group * 16 + 16, :] = values.reshape(32, 16, NY)

    bypass(0)

    fetch_owner.wait()
    summed = jnp.zeros((256, 128), F32)
    for dy in (0, 1, 3, 2):
        for dx in range(4):
            if dx or dy:
                slot = ys[dy] * 4 + xs[dx]
                arrived(0, slot, got_a.at[slot])
        summed += jnp.dot(
            to_owner[...], got_a[pl.ds(ys[dy] * 4, 4)].reshape(256, 128), preferred_element_type=F32
        )
    send_b[...] = summed.astype(BF16).reshape(16, 16, 128)

    send_line(1, send_b, got_b)
    got_b[line_me] = send_b[line_me]
    bypass(1)
    for copy in fetch_center:
        copy.wait()

    for index, _ in line:
        arrived(1, index, got_b.at[index])
    pencils = lax.dot_general(
        channels[...], got_b[...].reshape(256, 128), NT, preferred_element_type=F32
    ).astype(BF16)
    rows = []
    for part in range(2):
        for j in range(4):
            rows.append([])
    for block in range(4):
        real_at, imag_at = block * 256, 1024 + block * 256
        real = jnp.dot(pencils, table_z[0, :, real_at : real_at + 256], preferred_element_type=F32)
        real += jnp.dot(pencils, table_z[1, :, real_at : real_at + 256], preferred_element_type=F32)
        imag = jnp.dot(pencils, table_z[0, :, imag_at : imag_at + 256], preferred_element_type=F32)
        imag += jnp.dot(pencils, table_z[1, :, imag_at : imag_at + 256], preferred_element_type=F32)
        for j in range(4):
            weight_real = weight[j, 0, :, real_at : real_at + 256].astype(F32)
            weight_imag = weight[j, 1, :, real_at : real_at + 256].astype(F32)
            one, two = real[j * 32 : j * 32 + 32], imag[j * 32 : j * 32 + 32]
            rows[j].append(jnp.sum(one * weight_real - two * weight_imag, axis=0, keepdims=True))
            rows[4 + j].append(jnp.sum(one * weight_imag + two * weight_real, axis=0, keepdims=True))
    mixed = jnp.concatenate([jnp.concatenate(row, axis=1) for row in rows], axis=0)
    mixed = jnp.concatenate([mixed[:, h * 128 : h * 128 + 128] for h in range(8)], axis=0)
    turned = jnp.dot(mixed.astype(BF16), turn[...], preferred_element_type=F32)
    turned = jnp.concatenate([turned[:, t * 128 : t * 128 + 128] for t in range(4)], axis=0)
    row = lax.broadcasted_iota(jnp.int32, (256, 128), 0)
    lane = lax.broadcasted_iota(jnp.int32, (256, 128), 1)
    turned = jnp.where(lax.rem(row, 4) == lax.rem(lax.div(lane, 4), 4), turned, 0.0).astype(BF16)
    planes = jnp.dot(back_z[0], turned, preferred_element_type=F32)
    planes += jnp.dot(back_z[1], turned, preferred_element_type=F32)
    back_b[...] = planes.astype(BF16).reshape(16, 16, 128)

    send_line(2, back_b, home_b)
    home_b[line_me] = back_b[line_me]

    for index, _ in line:
        arrived(2, index, home_b.at[index])
    home = jnp.dot(to_grid[...], home_b[...].reshape(256, 128), preferred_element_type=F32)
    back_a[...] = home.astype(BF16).reshape(4, 64, 128)

    send_plane(3, lambda index: back_a.at[lax.shift_right_logical(index, 2)], home_a)
    home_a[arrival] = back_a[x]

    def store(b, group):
        rows = pl.ds(group * 4, 4)
        return pltpu.make_async_copy(result.at[b, rows], out_ref.at[b, rows], store_sems.at[b, group])

    lines = (lines_first, lines_second)

    def inverse_y_part(b, dy):
        rows = jnp.concatenate(
            [
                home_a[pl.ds(ys[dy] * 4, 4), at : at + 16, :].reshape(64, 128)
                for at in (b * 32, b * 32 + 16)
            ],
            axis=1,
        )
        rows = jnp.concatenate([rows, rows], axis=0)
        values = lax.dot_general(rows, back_y[...], TN, preferred_element_type=F32).astype(BF16)
        for half in range(2):
            for part in range(2):
                at = pl.multiple_of((part * 8 + half * 4 + ys[dy]) * 16, 16)
                for group in range(8):
                    row = half * 128 + group * 16
                    lines[b][group, pl.ds(at, 16), :] = values[
                        row : row + 16, part * NY : (part + 1) * NY
                    ]

    def finish(b, group):
        values = jnp.dot(back_x[...], lines[b][group], preferred_element_type=F32)
        channels = slice(group * 4, group * 4 + 4)
        total = values[:256] + values[256:] + direct[b, channels].reshape(256, NY)
        total = 0.5 * total * (1.0 + lax.erf(total * (1.0 / math.sqrt(2.0))))
        result[b, channels] = total.astype(BF16).reshape(4, 64, NY)
        store(b, group).start()

    near = (0, 1, 3, 2)
    for dy in near:
        for dx in range(4):
            if dx or dy:
                slot = ys[dy] * 4 + xs[dx]
                arrived(3, slot, home_a.at[slot])
        inverse_y_part(0, dy)
    for group in range(8):
        if group % 2 == 0:
            inverse_y_part(1, near[group // 2])
        finish(0, group)
    for group in range(8):
        finish(1, group)
    for copy in sent:
        copy.wait_send()

    def stored(group, carry):
        for b in range(2):
            store(b, group).wait()
        return carry

    lax.fori_loop(0, 8, stored, 0)


def hand_over_kernel(source_ref, out_ref, held, load_sems, store_sems):
    def load(part):
        at = (part // 4, pl.ds(part % 4 * 8, 8))
        return pltpu.make_async_copy(source_ref.at[at], held.at[at], load_sems.at[part])

    def store(part):
        at = (part // 4, pl.ds(part % 4 * 8, 8))
        return pltpu.make_async_copy(held.at[at], out_ref.at[at], store_sems.at[part])

    for part in range(8):
        load(part).start()
    for part in range(8):
        load(part).wait()
        store(part).start()
    for part in range(8):
        store(part).wait()


VMEM = pl.BlockSpec(memory_space=pltpu.VMEM)
HBM = pl.BlockSpec(memory_space=pltpu.HBM)


def shards(field, spectral_weight, bypass_weight, bypass_bias):
    result = pl.pallas_call(
        exchange_kernel,
        out_shape=jax.ShapeDtypeStruct(field.shape, BF16),
        in_specs=[HBM] * 12 + [VMEM] * 2,
        out_specs=HBM,
        scratch_shapes=[
            pltpu.VMEM((16, 64, 128), BF16),
            pltpu.VMEM((16, 64, 128), BF16),
            pltpu.VMEM((16, 16, 128), BF16),
            pltpu.VMEM((16, 16, 128), BF16),
            pltpu.VMEM((16, 16, 128), BF16),
            pltpu.VMEM((16, 16, 128), BF16),
            pltpu.VMEM((4, 64, 128), BF16),
            pltpu.VMEM((16, 64, 128), BF16),
            pltpu.VMEM((2, 32, 64, NY), BF16),
            pltpu.VMEM((2, 256, 256), BF16),
            pltpu.VMEM((64, 2 * NY), BF16),
            pltpu.VMEM((2048, 2 * NY), BF16),
            pltpu.VMEM((4, 2, 32, 1024), BF16),
            pltpu.VMEM((256, 256), BF16),
            pltpu.VMEM((128, 128), BF16),
            pltpu.VMEM((2, 256, 2048), BF16),
            pltpu.VMEM((128, 512), BF16),
            pltpu.VMEM((2, 256, 256), BF16),
            pltpu.VMEM((256, 256), BF16),
            pltpu.VMEM((128, 512), BF16),
            pltpu.VMEM((512, 256), BF16),
            pltpu.VMEM((512, 512), BF16),
            pltpu.VMEM((2, 32, 64, NY), F32),
            pltpu.VMEM((8, 256, NY), BF16),
            pltpu.VMEM((8, 256, NY), BF16),
            pltpu.VMEM((2, 32, 64, NY), BF16),
            pltpu.SemaphoreType.DMA((15,)),
            pltpu.SemaphoreType.DMA((4, 16)),
            pltpu.SemaphoreType.DMA((4, 16)),
            pltpu.SemaphoreType.DMA((2, 8)),
        ],
        compiler_params=pltpu.CompilerParams(
            collective_id=0, has_side_effects=True, vmem_limit_bytes=60 << 20
        ),
        name="exchange",
    )(
        field, jnp.asarray(forward_x()), jnp.asarray(forward_y()),
        spectral_weight, jnp.asarray(order_to_owner()), jnp.asarray(order_channels()),
        jnp.asarray(forward_z()), jnp.asarray(turn_lanes()), jnp.asarray(inverse_z()),
        jnp.asarray(order_to_grid()), jnp.asarray(inverse_y()), jnp.asarray(inverse_x()),
        bypass_weight, bypass_bias.reshape(1, 32),
    )

    return pl.pallas_call(
        hand_over_kernel,
        out_shape=jax.ShapeDtypeStruct(field.shape, BF16),
        in_specs=[HBM],
        out_specs=HBM,
        scratch_shapes=[
            pltpu.VMEM((2, 32, 64, NY), BF16),
            pltpu.SemaphoreType.DMA((8,)),
            pltpu.SemaphoreType.DMA((8,)),
        ],
        compiler_params=pltpu.CompilerParams(vmem_limit_bytes=60 << 20),
        name="hand_over",
    )(result)


def solution(mesh):
    in_specs = (P("gz", None, "gx", None), P(("gz", "gx"), None, None, None), P(), P())
    out_specs = P("gz", None, "gx", None)
    return jax.shard_map(shards, mesh=mesh, in_specs=in_specs, out_specs=out_specs, check_vma=False)
```
